32 devices in a mesh: dp: 8 (over z, core), seq: 4 (over y, x).
Axes of the slice: x: 2, y: 2, z: 4, core: 2. Of those that a mesh axis runs over, the one named last changes fastest.
Arguments:
- query_rows: bfloat16 [8, 512, 2048], P('dp', 'seq'), may hold values from -16 to 16
- key_rows: bfloat16 [8, 512, 2048], P('dp', 'seq'), may hold values from -16 to 16
- value_rows: bfloat16 [8, 512, 2048], P('dp', 'seq'), may hold values from -6 to 6
- out_cotangent: bfloat16 [8, 512, 2048], P('dp', 'seq'), may hold values from -6 to 6
- segment_ids: int32 [8, 512], P('dp'), may hold values from 0 to 7, never falling along the last dimension, each value on 1 to 384 neighbouring positions
- gain_query: float32 [16, 128], P('seq'), may hold values from 0.5 to 6
- gain_key: float32 [16, 128], P('seq'), may hold values from 0.5 to 6
Outputs:
- attended: bfloat16 [8, 512, 2048], P('dp', 'seq')
- grad_query: bfloat16 [8, 512, 2048], P('dp', 'seq')
- grad_key: bfloat16 [8, 512, 2048], P('dp', 'seq')
- grad_value: bfloat16 [8, 512, 2048], P('dp', 'seq')
- grad_gain_query: float32 [16, 128], P('seq')
- grad_gain_key: float32 [16, 128], P('seq')
The draws below stay inside these ranges and needn't reach their ends.
Inputs may be any that keep to these rules, and one draw needn't show every extreme that they name: `segment_ids`: image number of each token, never falling along the pack; each image with its prompt has 1 to 384 tokens, one exactly 384.
All inputs are finite; a program needn't handle non-finite values.
Results may differ from the reference program's by a relative error of at most 0.0065.
The reference program's roundings to bfloat16 on the way (of `weights_low` and `grad_scores`) count: a program that leaves them out, or rounds other values in their place, can miss the bound.
Values may be sent and summed in bfloat16 or wider, within the bound.
No kernel may reach another device: no remote copies, remote signals or barrier semaphores. Data moves between devices by JAX's collectives and lax.ppermute only.
A program may use at most 64 MiB of HBM per device.

```python
import math
import jax
import jax.numpy as jnp
import numpy as np
from jax import lax

HD = 128
HEADS = 16
IMAGES = 8
PACK_LEN = 512
PACKS = 8
MOST = 384


def drawn_rows(key):
    return jnp.clip(jax.random.normal(key, (PACKS, PACK_LEN, HEADS * HD), jnp.float32), -6.0, 6.0)


def draw_query_rows(key, part):
    key = jax.random.fold_in(key, 11)
    rows = drawn_rows(key)
    return rows.astype(jnp.bfloat16)


def draw_key_rows(key, part):
    key = jax.random.fold_in(key, 23)
    rows = drawn_rows(key)
    return rows.astype(jnp.bfloat16)


def gain_table(key):
    values = jnp.exp(jax.random.uniform(key, (HEADS, HD), jnp.float32, math.log(0.5), math.log(2.0)))
    return values


def draw_gain_query(key, part):
    key = jax.random.fold_in(key, 31)
    return gain_table(key)


def draw_gain_key(key, part):
    key = jax.random.fold_in(key, 47)
    return gain_table(key)


def steps_of(own_key, shape, split, smallest, top_value):
    factor_of, own = 1.0, jax.random.fold_in(own_key, 6)
    for position, blocks in split:
        heights = jnp.exp(jax.random.uniform(jax.random.fold_in(own, position), (blocks,), jnp.float32, smallest / len(split), top_value / len(split)))
        factor_of = factor_of * jnp.repeat(heights, shape[position] // blocks).reshape([-1 if axis == position else 1 for axis in range(len(shape))])
    return factor_of


def profile(amount, total, reach, slope):
    loads = [(1 << 20) // math.isqrt(standing ** slope) + 1 for standing in range(2, amount + 1)]
    rest, given = total - reach - (amount - 1), [1] * (amount - 1)
    while rest > 0:
        candidates = [i for i in range(amount - 1) if given[i] < reach]
        whole, budget = sum([loads[i] for i in candidates]), rest
        for i in candidates:
            addition = min(reach - given[i], max(1, budget * loads[i] // whole), rest)
            given[i] = given[i] + addition
            rest = rest - addition
    return np.array([reach] + given)


def uneven(key, number_of, total, reach, lean):
    if number_of == 2:
        one = jax.random.randint(key, (), max(1, total - reach), min(reach, total - 1) + 1)
        return jnp.stack([one, total - one])
    sizes = jnp.asarray(profile(number_of, total, reach, lean), jnp.int32)
    twos = (number_of - 1) // 2
    source_of, sink = sizes[1:1 + 2 * twos:2], sizes[2:2 + 2 * twos:2]
    margin = jnp.minimum(source_of - 1, reach - sink)
    moved = jax.random.randint(jax.random.fold_in(key, 1), (twos,), 0, 1 << 20) % (margin + 1)
    sizes = sizes.at[1:1 + 2 * twos:2].set(source_of - moved).at[2:2 + 2 * twos:2].set(sink + moved)
    return sizes[jax.random.permutation(jax.random.fold_in(key, 2), number_of)]


def bell_draw(stream_key, extent, deviation, limit, shards=(), kind=jnp.bfloat16):
    result = jax.random.normal(stream_key, extent, jnp.float32) * deviation
    if len(shards) > 0:
        result = steps_of(stream_key, extent, shards, -0.22, 0.18) * result
    return jnp.clip(result, min=-limit, max=limit).astype(kind)


def setup_inputs(seed: int = 0) -> dict:
    key_of = jax.random.split(jax.random.key(seed), 8)
    query_rows = draw_query_rows(jax.random.fold_in(key_of[7], 71), 0)
    key_rows = draw_key_rows(jax.random.fold_in(key_of[7], 71), 0)
    value_rows = bell_draw(key_of[2], (PACKS, PACK_LEN, HEADS * HD), 1.0, 6.0, ((0, 8), (1, 4)))
    out_cotangent = bell_draw(key_of[3], (PACKS, PACK_LEN, HEADS * HD), 1.0, 6.0, ((0, 8), (1, 4)))
    segment_ids = jax.vmap(lambda own: jnp.searchsorted(jnp.cumsum(uneven(own, IMAGES, PACK_LEN, MOST, 2)), jnp.arange(PACK_LEN), side="right"))(jax.random.split(key_of[4], PACKS)).reshape((PACKS, PACK_LEN)).astype(jnp.int32)
    gain_query = draw_gain_query(jax.random.fold_in(key_of[7], 71), 0)
    gain_key = draw_gain_key(jax.random.fold_in(key_of[7], 71), 0)
    return dict(query_rows=query_rows, key_rows=key_rows, value_rows=value_rows, out_cotangent=out_cotangent, segment_ids=segment_ids, gain_query=gain_query, gain_key=gain_key)


NEGATIVE = -1e+30
EPSILON = 1e-06

def normalize(rows, gain):
    inverse = lax.rsqrt(lax.optimization_barrier(jnp.mean(rows * rows, axis=-1, keepdims=True)) + EPSILON)
    return rows * inverse * gain

def one_head(pieces):
    queries, keys_all, values_all, grads_out, segments, gain_row, gain_col = pieces
    score_scale = 1.0 / math.sqrt(HD)
    query_norm32, query_back = jax.vjp(normalize, queries.astype(jnp.float32), gain_row)
    key_norm32, key_back = jax.vjp(normalize, keys_all.astype(jnp.float32), gain_col)
    query_norm = query_norm32.astype(jnp.bfloat16)
    key_norm = key_norm32.astype(jnp.bfloat16)
    scores = jnp.dot(query_norm, key_norm.T, preferred_element_type=jnp.float32) * score_scale
    allowed = segments[:, None] == segments[None, :]
    row_max = lax.optimization_barrier(jnp.max(jnp.where(allowed, scores, NEGATIVE), axis=1))
    shifted = jnp.where(allowed, jnp.exp(scores - row_max[:, None]), 0.0)
    weights = shifted / lax.optimization_barrier(jnp.sum(shifted, axis=1))[:, None]
    weights_low = weights.astype(jnp.bfloat16)
    output_full = jnp.dot(weights_low, values_all, preferred_element_type=jnp.float32)
    attended = output_full.astype(jnp.bfloat16)
    grad_probs = jnp.dot(grads_out, values_all.T, preferred_element_type=jnp.float32)
    row_delta = lax.optimization_barrier(jnp.sum(grads_out.astype(jnp.float32) * output_full, axis=1))
    grad_scores = (weights * (grad_probs - row_delta[:, None])).astype(jnp.bfloat16)
    query_grad_norm = jnp.dot(grad_scores, key_norm, preferred_element_type=jnp.float32) * score_scale
    key_grad_norm = jnp.dot(grad_scores.T, query_norm, preferred_element_type=jnp.float32) * score_scale
    value_grad = jnp.dot(weights_low.T, grads_out, preferred_element_type=jnp.float32).astype(jnp.bfloat16)
    query_grad, gain_grad_q = query_back(query_grad_norm)
    key_grad, gain_grad_k = key_back(key_grad_norm)
    return (attended, query_grad.astype(jnp.bfloat16), key_grad.astype(jnp.bfloat16), value_grad, gain_grad_q, gain_grad_k)

def reference(query_rows, key_rows, value_rows, out_cotangent, segment_ids, gain_query, gain_key):

    def by_head(array):
        return array.reshape(PACKS, PACK_LEN, HEADS, HD).transpose(0, 2, 1, 3).reshape(PACKS * HEADS, PACK_LEN, HD)

    def by_token(array):
        return array.reshape(PACKS, HEADS, PACK_LEN, HD).transpose(0, 2, 1, 3).reshape(PACKS, PACK_LEN, HEADS * HD)
    seg_rows = jnp.broadcast_to(segment_ids[:, None, :], (PACKS, HEADS, PACK_LEN)).reshape(PACKS * HEADS, PACK_LEN)
    gains_q = jnp.broadcast_to(gain_query[None], (PACKS, HEADS, HD)).reshape(PACKS * HEADS, HD)
    gains_k = jnp.broadcast_to(gain_key[None], (PACKS, HEADS, HD)).reshape(PACKS * HEADS, HD)
    results = lax.map(one_head, (by_head(query_rows), by_head(key_rows), by_head(value_rows), by_head(out_cotangent), seg_rows, gains_q, gains_k))
    attended, query_grad, key_grad, value_grad, gain_grad_q, gain_grad_k = results
    return (by_token(attended), by_token(query_grad), by_token(key_grad), by_token(value_grad), lax.optimization_barrier(jnp.sum(gain_grad_q.reshape(PACKS, HEADS, HD), axis=0)), lax.optimization_barrier(jnp.sum(gain_grad_k.reshape(PACKS, HEADS, HD), axis=0)))
```

```python
import functools
import math

import jax
import jax.numpy as jnp
from jax import lax
from jax.experimental import pallas as pl
from jax.experimental.pallas import tpu as pltpu
from jax.sharding import PartitionSpec as P

NEGATIVE = -1e30
EPSILON = 1e-06
VMEM_LIMIT = 48 * 1024 * 1024
ANY = pl.BlockSpec(memory_space=pl.ANY)
HBM = pl.BlockSpec(memory_space=pltpu.HBM)
WHOLE = pl.BlockSpec(memory_space=pltpu.VMEM)


def run_copies(copies):
    for copy in copies:
        copy.start()
    for copy in copies:
        copy.wait()


def head_columns(owner, local_width, first, width):
    return pl.ds(pl.multiple_of(owner * local_width + first, 128), width)


def flipped(k, shards):
    bits = shards.bit_length() - 1
    if bits % 2:
        return k
    low = (1 << bits // 2) - 1
    return (k & low) << bits // 2 | k >> bits // 2


def partner_of(k, shards):
    odd = lax.axis_index("dp") & 1
    return lax.axis_index("seq") ^ (k + odd * (flipped(k, shards) - k))


def pack_kernel(shards, local_width, first, width, *refs):
    rows, outs, sems = refs[:4], refs[4:-1], refs[-1]
    run_copies(
        [
            pltpu.make_async_copy(
                rows[a].at[0, :, head_columns(partner_of(k, shards), local_width, first, width)],
                out.at[a],
                sems.at[k, a],
            )
            for k, out in enumerate(outs, start=1)
            for a in range(4)
        ]
    )


def pack(shards, local_width, first, width, rows):
    shape = jax.ShapeDtypeStruct((4, rows[0].shape[1], width), rows[0].dtype)
    moved = (shards - 1) * math.prod(shape.shape) * 4
    return pl.pallas_call(
        functools.partial(pack_kernel, shards, local_width, first, width),
        out_shape=[shape] * (shards - 1),
        in_specs=[HBM] * 4,
        out_specs=[ANY] * (shards - 1),
        scratch_shapes=[pltpu.SemaphoreType.DMA((shards, 4))],
        compiler_params=pltpu.CompilerParams(vmem_limit_bytes=VMEM_LIMIT),
        cost_estimate=pl.CostEstimate(flops=0, bytes_accessed=moved, transcendentals=0),
        name="pack",
    )(*rows)


def unpack_kernel(shards, local_width, first, width, held, *refs):
    pieces, outs, sems = refs[:shards], refs[shards + held : -1], refs[-1]
    run_copies(
        [
            pltpu.make_async_copy(
                pieces[k].at[a],
                outs[a].at[0, :, head_columns(partner_of(k, shards), local_width, first, width)],
                sems.at[k, a],
            )
            for k in range(shards)
            for a in range(4)
        ]
    )


def unpack(shards, local_width, first, width, pieces, held):
    tokens = pieces[0].shape[1]
    shape = jax.ShapeDtypeStruct((1, tokens, shards * local_width), pieces[0].dtype)
    moved = sum(piece.size for piece in pieces) * 4
    return pl.pallas_call(
        functools.partial(unpack_kernel, shards, local_width, first, width, len(held)),
        out_shape=[shape] * 4,
        in_specs=[ANY] * (shards + len(held)),
        out_specs=[ANY] * 4,
        input_output_aliases={shards + a: a for a in range(len(held))},
        scratch_shapes=[pltpu.SemaphoreType.DMA((shards, 4))],
        compiler_params=pltpu.CompilerParams(vmem_limit_bytes=VMEM_LIMIT),
        cost_estimate=pl.CostEstimate(flops=0, bytes_accessed=moved, transcendentals=0),
        name="unpack",
    )(*pieces, *held)


def dot_nn(left, right):
    return lax.dot_general(
        left, right, (((1,), (0,)), ((), ())), preferred_element_type=jnp.float32
    )


def dot_nt(left, right):
    return lax.dot_general(
        left, right, (((1,), (1,)), ((), ())), preferred_element_type=jnp.float32
    )


def dot_tn(left, right):
    return lax.dot_general(
        left, right, (((0,), (0,)), ((), ())), preferred_element_type=jnp.float32
    )


def norm_forward(rows, gain):
    inverse = lax.rsqrt(jnp.mean(rows * rows, axis=1, keepdims=True) + EPSILON)
    unit = rows * inverse
    return (unit * gain).astype(jnp.bfloat16), unit, inverse


def norm_backward(grads, unit, inverse, gain, score_scale):
    scaled = grads * (gain * score_scale)
    along = jnp.mean(scaled * unit, axis=1, keepdims=True)
    gain_grad = jnp.sum(grads * unit, axis=0, keepdims=True) * score_scale
    return inverse * (scaled - unit * along), gain_grad


def attend(queries, keys, values, grads, gain_q, gain_k, allowed, block, score_scale):
    query_norm, query_unit, query_inverse = norm_forward(queries, gain_q)
    key_norm, key_unit, key_inverse = norm_forward(keys, gain_k)
    values = values.astype(jnp.bfloat16)
    grads = grads.astype(jnp.bfloat16)
    outs, query_grads = [], []
    key_grad = value_grad = None
    exponent_scale = score_scale * math.log2(math.e)
    for start in range(0, queries.shape[0], block):
        rows = slice(start, start + block)
        query_block, grads_block = query_norm[rows], grads[rows]
        scores = dot_nt(key_norm, query_block)
        if allowed is not None:
            scores = jnp.where(allowed, scores, NEGATIVE)
        row_max = jnp.max(scores, axis=0, keepdims=True)
        shifted = jnp.exp2((scores - row_max) * exponent_scale)
        if allowed is not None:
            shifted = jnp.where(allowed, shifted, 0.0)
        weights = shifted * (1.0 / jnp.sum(shifted, axis=0, keepdims=True))
        weights_low = weights.astype(jnp.bfloat16)
        output = dot_tn(values, weights_low)
        grads_turned = grads_block.astype(jnp.float32).T
        row_delta = jnp.sum(grads_turned * output, axis=0, keepdims=True)
        grad_probs = dot_nt(values, grads_block)
        grad_scores = (weights * (grad_probs - row_delta)).astype(jnp.bfloat16)
        outs.append(output.T)
        query_grads.append(dot_tn(key_norm, grad_scores).T)
        value_part = dot_nn(weights_low, grads_block)
        key_part = dot_nn(grad_scores, query_block)
        value_grad = value_part if value_grad is None else value_grad + value_part
        key_grad = key_part if key_grad is None else key_grad + key_part
    join = lambda parts: parts[0] if len(parts) == 1 else jnp.concatenate(parts, axis=0)
    query_grad, gain_grad_q = norm_backward(
        join(query_grads), query_unit, query_inverse, gain_q, score_scale
    )
    key_grad, gain_grad_k = norm_backward(key_grad, key_unit, key_inverse, gain_k, score_scale)
    return (join(outs), query_grad, key_grad, value_grad), (gain_grad_q, gain_grad_k)


def attention_kernel(shards, first, heads, has_held, *refs):
    own, refs = refs[:4], refs[4:]
    received, refs = refs[: shards - 1], refs[shards - 1 :]
    (seg_ref, gain_q_ref, gain_k_ref), refs = refs[:3], refs[3:]
    if has_held:
        held_ref, refs = refs[0], refs[1:]
    sent, refs = refs[:shards], refs[shards:]
    gains_ref, inputs, results, in_sems, out_sems = refs
    me = lax.axis_index("seq")
    tokens, head_dim = own[0].shape[1], gain_q_ref.shape[1]
    local_width = gain_q_ref.shape[0] * head_dim
    width = heads * head_dim
    length = shards * tokens
    quarter = length // 4
    score_scale = 1.0 / math.sqrt(head_dim)

    def place(k):
        return pl.ds(pl.multiple_of(partner_of(k, shards) * tokens, tokens), tokens)

    own_columns = head_columns(me, local_width, first * head_dim, width)
    copies = [
        pltpu.make_async_copy(
            own[a].at[0, :, own_columns], inputs.at[a, place(0), :], in_sems.at[0, a]
        )
        for a in range(4)
    ]
    copies += [
        pltpu.make_async_copy(
            received[k - 1].at[a], inputs.at[a, place(k), :], in_sems.at[k, a]
        )
        for k in range(1, shards)
        for a in range(4)
    ]
    for copy in copies:
        copy.start()

    segments = seg_ref[...].astype(jnp.float32)
    lane = lax.broadcasted_iota(jnp.int32, (1, length), 1)
    middle = jnp.max(jnp.where(lane == length // 2, segments, -1.0), axis=1, keepdims=True)
    before = jnp.sum(jnp.where(segments < middle, 1.0, 0.0), axis=1, keepdims=True)
    row = lax.broadcasted_iota(jnp.int32, (quarter, head_dim), 0).astype(jnp.float32)
    late = row >= before
    late_lanes = lane[:, :quarter].astype(jnp.float32) >= before
    seg_rest = jnp.where(late_lanes, segments[:, 3 * quarter :], segments[:, :quarter])
    seg_lanes = jnp.broadcast_to(seg_rest, (quarter, quarter))
    allowed = seg_lanes == seg_lanes.T

    for copy in copies:
        copy.wait()

    for head in range(heads):
        columns = slice(head * head_dim, (head + 1) * head_dim)
        image, rest = [], []
        for a in range(4):
            early = inputs[a, :quarter, columns].astype(jnp.float32)
            latest = inputs[a, 3 * quarter :, columns].astype(jnp.float32)
            middle_rows = inputs[a, quarter : 3 * quarter, columns].astype(jnp.float32)
            image.append(jnp.concatenate([jnp.where(late, early, latest), middle_rows], axis=0))
            rest.append(jnp.where(late, latest, early))
        gain_q = gain_q_ref[first + head : first + head + 1, :]
        gain_k = gain_k_ref[first + head : first + head + 1, :]
        block = min(3 * quarter, 384)
        image_out, image_gains = attend(*image, gain_q, gain_k, None, block, score_scale)
        rest_out, rest_gains = attend(*rest, gain_q, gain_k, allowed, quarter, score_scale)
        for a in range(4):
            shared, other = image_out[a][:quarter], rest_out[a]
            results[a, :quarter, columns] = jnp.where(late, shared, other).astype(jnp.bfloat16)
            results[a, quarter : 3 * quarter, columns] = image_out[a][quarter:].astype(jnp.bfloat16)
            results[a, 3 * quarter :, columns] = jnp.where(late, other, shared).astype(jnp.bfloat16)
        for side in range(2):
            gains_ref[side, first + head : first + head + 1, :] = image_gains[side] + rest_gains[side]
    if has_held:
        gains_ref[:, :first, :] = held_ref[:, :first, :]

    run_copies(
        [
            pltpu.make_async_copy(
                results.at[a, place(k), :], sent[k].at[a], out_sems.at[k, a]
            )
            for k in range(shards)
            for a in range(4)
        ]
    )


def attention(shards, first, heads, rows, received, segments, gain_q, gain_k, held):
    tokens, head_dim = rows[0].shape[1], gain_q.shape[1]
    width, length = heads * head_dim, shards * tokens
    pieces = [jax.ShapeDtypeStruct((4, tokens, width), jnp.bfloat16)] * shards
    gains = jax.ShapeDtypeStruct((2,) + gain_q.shape, jnp.float32)
    cost = pl.CostEstimate(
        flops=12 * heads * length * length * head_dim,
        bytes_accessed=16 * length * width,
        transcendentals=heads * length * length,
    )
    return pl.pallas_call(
        functools.partial(attention_kernel, shards, first, heads, len(held) > 0),
        out_shape=pieces + [gains],
        in_specs=[HBM] * 4 + [ANY] * len(received) + [WHOLE] * (3 + len(held)),
        out_specs=[ANY] * len(pieces) + [WHOLE],
        scratch_shapes=[
            pltpu.VMEM((4, length, width), jnp.bfloat16),
            pltpu.VMEM((4, length, width), jnp.bfloat16),
            pltpu.SemaphoreType.DMA((shards, 4)),
            pltpu.SemaphoreType.DMA((shards, 4)),
        ],
        compiler_params=pltpu.CompilerParams(vmem_limit_bytes=VMEM_LIMIT),
        cost_estimate=cost,
        name="attention",
    )(*rows, *received, segments, gain_q, gain_k, *held)


def exchange(array, axis, size, k):
    return lax.ppermute(array, axis, [(i, i ^ k) for i in range(size)])


def exchange_slots(pieces, packs, shards):
    arrived = []
    for k, piece in enumerate(pieces, start=1):
        pairs = [
            (pack * shards + i, pack * shards + (i ^ (flipped(k, shards) if pack % 2 else k)))
            for pack in range(packs)
            for i in range(shards)
        ]
        arrived.append(lax.ppermute(piece, ("dp", "seq"), pairs))
    return arrived


def on_device(shards, packs, query_rows, key_rows, value_rows, out_cotangent, segment_ids, gain_query, gain_key):
    rows = tuple(
        pltpu.with_memory_space_constraint(array, pltpu.HBM)
        for array in (query_rows, key_rows, value_rows, out_cotangent)
    )
    local_heads, head_dim = gain_query.shape
    local_width = local_heads * head_dim
    heads = local_heads // 2 if local_heads % 2 == 0 else local_heads
    firsts = range(0, local_heads, heads)
    width = heads * head_dim
    arrived = []
    for first in firsts:
        packed = pack(shards, local_width, first * head_dim, width, rows)
        arrived.append(exchange_slots(packed, packs, shards))
    gains = ()
    returned = []
    for first, received in zip(firsts, arrived):
        *pieces, gains = attention(
            shards, first, heads, rows, received, segment_ids, gain_query, gain_key, gains
        )
        gains = (gains,)
        returned.append(pieces[:1] + exchange_slots(pieces[1:], packs, shards))
    total, step = gains[0], 1
    while step < packs:
        waited = slice(0, -1) if step == 1 else slice(-1, None)
        if step <= 2:
            total, returned[0][waited] = lax.optimization_barrier((total, returned[0][waited]))
        total = total + exchange(total, "dp", packs, step)
        step *= 2
    sums = (total[0], total[1])
    sums, returned[-1][0] = lax.optimization_barrier((sums, returned[-1][0]))
    outs = ()
    for first, pieces in zip(firsts, returned):
        outs = unpack(shards, local_width, first * head_dim, width, pieces, outs)
    return (*outs, *sums)


def solution(mesh):
    rows = P("dp", "seq", None)
    gain = P("seq", None)
    return jax.shard_map(
        functools.partial(on_device, mesh.shape["seq"], mesh.shape["dp"]),
        mesh=mesh,
        in_specs=(rows, rows, rows, rows, P("dp", None), gain, gain),
        out_specs=(rows, rows, rows, rows, gain, gain),
        check_vma=False,
    )
```

```python
import functools
import math

import jax
import jax.numpy as jnp
from jax import lax
from jax.experimental import pallas as pl
from jax.experimental.pallas import tpu as pltpu
from jax.sharding import PartitionSpec as P

NEGATIVE = -1e30
EPSILON = 1e-06
VMEM_LIMIT = 48 * 1024 * 1024
ANY = pl.BlockSpec(memory_space=pl.ANY)
HBM = pl.BlockSpec(memory_space=pltpu.HBM)
WHOLE = pl.BlockSpec(memory_space=pltpu.VMEM)


def run_copies(copies):
    for copy in copies:
        copy.start()
    for copy in copies:
        copy.wait()


def head_columns(owner, local_width, first, width):
    return pl.ds(pl.multiple_of(owner * local_width + first, 128), width)


def partners(k, shards):
    if shards == 4:
        return ((0, 0), (1, 3), (2, 1), (3, 2))[k]
    bits = shards.bit_length() - 1
    low = (1 << bits // 2) - 1
    return (k, k if bits % 2 else (k & low) << bits // 2 | k >> bits // 2)


def partner_of(k, shards):
    even, odd = partners(k, shards)
    return lax.axis_index("seq") ^ (even + (lax.axis_index("dp") & 1) * (odd - even))


def pack_kernel(items, shards, local_width, width, *refs):
    rows, outs, sems = refs[:4], refs[4:-1], refs[-1]
    run_copies(
        [
            pltpu.make_async_copy(
                rows[a].at[0, :, head_columns(partner_of(k, shards), local_width, first, width)],
                outs[i].at[a],
                sems.at[i, a],
            )
            for i, (k, first) in enumerate(items)
            for a in range(4)
        ]
    )


def pack(items, shards, local_width, width, rows):
    shape = jax.ShapeDtypeStruct((4, rows[0].shape[1], width), rows[0].dtype)
    moved = len(items) * math.prod(shape.shape) * 4
    return pl.pallas_call(
        functools.partial(pack_kernel, items, shards, local_width, width),
        out_shape=[shape] * len(items),
        in_specs=[HBM] * 4,
        out_specs=[ANY] * len(items),
        scratch_shapes=[pltpu.SemaphoreType.DMA((len(items), 4))],
        compiler_params=pltpu.CompilerParams(vmem_limit_bytes=VMEM_LIMIT),
        cost_estimate=pl.CostEstimate(flops=0, bytes_accessed=moved, transcendentals=0),
        name="pack",
    )(*rows)


def unpack_kernel(slots, shards, local_width, first, width, held, *refs):
    pieces, outs, sems = refs[: len(slots)], refs[len(slots) + held : -1], refs[-1]
    run_copies(
        [
            pltpu.make_async_copy(
                piece.at[a],
                outs[a].at[0, :, head_columns(partner_of(k, shards), local_width, first, width)],
                sems.at[k, a],
            )
            for piece, k in zip(pieces, slots)
            for a in range(4)
        ]
    )


def unpack(slots, shards, local_width, first, width, pieces, held):
    tokens = pieces[0].shape[1]
    shape = jax.ShapeDtypeStruct((1, tokens, shards * local_width), pieces[0].dtype)
    moved = sum(piece.size for piece in pieces) * 4
    return pl.pallas_call(
        functools.partial(unpack_kernel, slots, shards, local_width, first, width, len(held)),
        out_shape=[shape] * 4,
        in_specs=[ANY] * (len(slots) + len(held)),
        out_specs=[ANY] * 4,
        input_output_aliases={len(slots) + a: a for a in range(len(held))},
        scratch_shapes=[pltpu.SemaphoreType.DMA((shards, 4))],
        compiler_params=pltpu.CompilerParams(vmem_limit_bytes=VMEM_LIMIT),
        cost_estimate=pl.CostEstimate(flops=0, bytes_accessed=moved, transcendentals=0),
        name="unpack",
    )(*pieces, *held)


def dot_nn(left, right):
    return lax.dot_general(
        left, right, (((1,), (0,)), ((), ())), preferred_element_type=jnp.float32
    )


def dot_nt(left, right):
    return lax.dot_general(
        left, right, (((1,), (1,)), ((), ())), preferred_element_type=jnp.float32
    )


def dot_tn(left, right):
    return lax.dot_general(
        left, right, (((0,), (0,)), ((), ())), preferred_element_type=jnp.float32
    )


def norm_forward(rows, gain, axis):
    inverse = lax.rsqrt(jnp.mean(rows * rows, axis=axis, keepdims=True) + EPSILON)
    unit = rows * inverse
    return (unit * gain).astype(jnp.bfloat16), unit, inverse


def norm_backward(grads, unit, inverse, gain, score_scale, axis):
    scaled = grads * (gain * score_scale)
    along = jnp.mean(scaled * unit, axis=axis, keepdims=True)
    gain_grad = jnp.sum(grads * unit, axis=1 - axis, keepdims=True) * score_scale
    return inverse * (scaled - unit * along), gain_grad


def attend(queries, keys, values, grads, gain_q, gain_k, allowed, block, score_scale):
    tokens = queries.shape[0]
    gain_q = jnp.concatenate([gain_q] * (tokens // gain_q.shape[1]), axis=1)
    turned = queries.T.astype(jnp.float32)
    query_norm, query_unit, query_inverse = norm_forward(turned, gain_q, 0)
    key_norm, key_unit, key_inverse = norm_forward(keys.astype(jnp.float32), gain_k, 1)
    keys_turned, values_turned, grads_turned = key_norm.T, values.T, grads.T
    outs, query_grads = [], []
    key_grad = value_grad = None
    exponent_scale = score_scale * math.log2(math.e)
    for start in range(0, tokens, block):
        span = slice(start, start + block)
        query_block, grads_block = query_norm[:, span], grads_turned[:, span]
        scores = dot_nn(key_norm, query_block)
        if allowed is not None:
            scores = jnp.where(allowed, scores, NEGATIVE)
        row_max = jnp.max(scores, axis=0, keepdims=True)
        shifted = jnp.exp2((scores - row_max) * exponent_scale)
        if allowed is not None:
            shifted = jnp.where(allowed, shifted, 0.0)
        weights = shifted * (1.0 / jnp.sum(shifted, axis=0, keepdims=True))
        weights_low = weights.astype(jnp.bfloat16)
        output = dot_nn(values_turned, weights_low)
        row_delta = jnp.sum(grads_block.astype(jnp.float32) * output, axis=0, keepdims=True)
        grad_probs = dot_nn(values, grads_block)
        grad_scores = (weights * (grad_probs - row_delta)).astype(jnp.bfloat16)
        outs.append(output.astype(jnp.bfloat16))
        query_grads.append(dot_nn(keys_turned, grad_scores))
        value_part = dot_nn(weights_low, grads[span])
        key_part = dot_nt(grad_scores, query_block)
        value_grad = value_part if value_grad is None else value_grad + value_part
        key_grad = key_part if key_grad is None else key_grad + key_part
    join = lambda parts: parts[0] if len(parts) == 1 else jnp.concatenate(parts, axis=1)
    query_grad, gain_grad_q = norm_backward(
        join(query_grads), query_unit, query_inverse, gain_q, score_scale, 0
    )
    key_grad, gain_grad_k = norm_backward(key_grad, key_unit, key_inverse, gain_k, score_scale, 1)
    results = (join(outs).T, query_grad.astype(jnp.bfloat16).T, key_grad, value_grad)
    return results, (gain_grad_q, gain_grad_k)


def attention_kernel(shards, first, heads, has_held, *refs):
    pieces, refs = refs[:shards], refs[shards:]
    (seg_ref, gain_q_ref, gain_k_ref), refs = refs[:3], refs[3:]
    if has_held:
        held_ref, refs = refs[0], refs[1:]
    sent, refs = refs[:shards], refs[shards:]
    gains_ref, inputs, results, in_sems, out_sems = refs
    tokens, head_dim = pieces[0].shape[1], gain_q_ref.shape[1]
    length = shards * tokens
    quarter = length // 4
    score_scale = 1.0 / math.sqrt(head_dim)

    def place(k):
        return pl.ds(pl.multiple_of(partner_of(k, shards) * tokens, tokens), tokens)

    copies = [
        pltpu.make_async_copy(pieces[k].at[a], inputs.at[a, place(k), :], in_sems.at[k, a])
        for k in range(shards)
        for a in range(4)
    ]
    for copy in copies:
        copy.start()

    segments = seg_ref[...].astype(jnp.float32)
    lane = lax.broadcasted_iota(jnp.int32, (1, length), 1)
    middle = jnp.max(jnp.where(lane == length // 2, segments, -1.0), axis=1, keepdims=True)
    before = jnp.sum(jnp.where(segments < middle, 1.0, 0.0), axis=1, keepdims=True)
    row = lax.broadcasted_iota(jnp.int32, (quarter, head_dim), 0).astype(jnp.float32)
    late = row >= before
    late_lanes = lane[:, :quarter].astype(jnp.float32) >= before
    seg_rest = jnp.where(late_lanes, segments[:, 3 * quarter :], segments[:, :quarter])
    seg_lanes = jnp.broadcast_to(seg_rest, (quarter, quarter))
    allowed = seg_lanes == seg_lanes.T

    def turn(row):
        return jnp.broadcast_to(row, (head_dim, head_dim)).T

    for copy in copies:
        copy.wait()

    for head in range(heads):
        columns = slice(head * head_dim, (head + 1) * head_dim)
        image, rest = [], []
        for a in range(4):
            early = inputs[a, :quarter, columns].astype(jnp.float32)
            latest = inputs[a, 3 * quarter :, columns].astype(jnp.float32)
            shared = jnp.where(late, early, latest).astype(jnp.bfloat16)
            image.append(jnp.concatenate([shared, inputs[a, quarter : 3 * quarter, columns]], axis=0))
            rest.append(jnp.where(late, latest, early).astype(jnp.bfloat16))
        own = slice(first + head, first + head + 1)
        gain_q, gain_k = turn(gain_q_ref[own, :]), gain_k_ref[own, :]
        block = min(3 * quarter, 384)
        image_out, image_gains = attend(*image, gain_q, gain_k, None, block, score_scale)
        rest_out, rest_gains = attend(*rest, gain_q, gain_k, allowed, quarter, score_scale)
        for a in range(4):
            shared = image_out[a][:quarter].astype(jnp.float32)
            other = rest_out[a].astype(jnp.float32)
            results[a, :quarter, columns] = jnp.where(late, shared, other).astype(jnp.bfloat16)
            results[a, quarter : 3 * quarter, columns] = image_out[a][quarter:].astype(jnp.bfloat16)
            results[a, 3 * quarter :, columns] = jnp.where(late, other, shared).astype(jnp.bfloat16)
        column = jnp.broadcast_to(image_gains[0] + rest_gains[0], (head_dim, head_dim))
        gains_ref[0, own, :] = column.T[:1]
        gains_ref[1, own, :] = image_gains[1] + rest_gains[1]
    if has_held:
        gains_ref[:, :first, :] = held_ref[:, :first, :]

    run_copies(
        [
            pltpu.make_async_copy(
                results.at[a, place(k), :], sent[k].at[a], out_sems.at[k, a]
            )
            for k in range(shards)
            for a in range(4)
        ]
    )


def attention(shards, first, heads, received, segments, gain_q, gain_k, held):
    tokens, head_dim = received[0].shape[1], gain_q.shape[1]
    width, length = heads * head_dim, shards * tokens
    pieces = [jax.ShapeDtypeStruct((4, tokens, width), jnp.bfloat16)] * shards
    gains = jax.ShapeDtypeStruct((2,) + gain_q.shape, jnp.float32)
    cost = pl.CostEstimate(
        flops=12 * heads * length * length * head_dim,
        bytes_accessed=16 * length * width,
        transcendentals=heads * length * length,
    )
    return pl.pallas_call(
        functools.partial(attention_kernel, shards, first, heads, len(held) > 0),
        out_shape=pieces + [gains],
        in_specs=[ANY] * shards + [WHOLE] * (3 + len(held)),
        out_specs=[ANY] * len(pieces) + [WHOLE],
        scratch_shapes=[
            pltpu.VMEM((4, length, width), jnp.bfloat16),
            pltpu.VMEM((4, length, width), jnp.bfloat16),
            pltpu.SemaphoreType.DMA((shards, 4)),
            pltpu.SemaphoreType.DMA((shards, 4)),
        ],
        compiler_params=pltpu.CompilerParams(vmem_limit_bytes=VMEM_LIMIT),
        cost_estimate=cost,
        name="attention",
    )(*received, segments, gain_q, gain_k, *held)


def exchange(array, axis, size, k):
    return lax.ppermute(array, axis, [(i, i ^ k) for i in range(size)])


def exchange_slots(pieces, packs, shards):
    arrived = []
    for k, piece in enumerate(pieces, start=1):
        pairs = [
            (pack * shards + i, pack * shards + (i ^ partners(k, shards)[pack % 2]))
            for pack in range(packs)
            for i in range(shards)
        ]
        arrived.append(lax.ppermute(piece, ("dp", "seq"), pairs))
    return arrived


def on_device(shards, packs, query_rows, key_rows, value_rows, out_cotangent, segment_ids, gain_query, gain_key):
    rows = tuple(
        pltpu.with_memory_space_constraint(array, pltpu.HBM)
        for array in (query_rows, key_rows, value_rows, out_cotangent)
    )
    local_heads, head_dim = gain_query.shape
    local_width = local_heads * head_dim
    heads = local_heads // 2 if local_heads % 2 == 0 else local_heads
    firsts = range(0, local_heads, heads)
    width = heads * head_dim
    arrived, kept = [], []
    for first in firsts:
        items = [(k, first * head_dim) for k in range(1, shards)]
        if first == firsts[-1]:
            items += [(0, start * head_dim) for start in firsts]
        packed = pack(items, shards, local_width, width, rows)
        arrived.append(exchange_slots(packed[: shards - 1], packs, shards))
        kept += packed[shards - 1 :]
    gains = ()
    returned = []
    for first, own, received in zip(firsts, kept, arrived):
        *pieces, gains = attention(
            shards, first, heads, [own] + received, segment_ids, gain_query, gain_key, gains
        )
        gains = (gains,)
        returned.append(pieces[:1] + exchange_slots(pieces[1:], packs, shards))
    total, step = gains[0], 1
    while step < packs:
        waited = slice(0, -1) if step == 1 else slice(-1, None)
        if step <= 2:
            total, returned[0][waited] = lax.optimization_barrier((total, returned[0][waited]))
        total = total + exchange(total, "dp", packs, step)
        step *= 2
    sums = (total[0], total[1])
    sums, returned[-1][0] = lax.optimization_barrier((sums, returned[-1][0]))
    outs = ()
    for first, pieces in zip(firsts, returned):
        slots = tuple(range(shards))
        parts = [slots[:-1], slots[-1:]] if first == firsts[-1] else [slots]
        for part in parts:
            some = [pieces[k] for k in part]
            outs = unpack(part, shards, local_width, first * head_dim, width, some, outs)
    return (*outs, *sums)


def solution(mesh):
    rows = P("dp", "seq", None)
    gain = P("seq", None)
    return jax.shard_map(
        functools.partial(on_device, mesh.shape["seq"], mesh.shape["dp"]),
        mesh=mesh,
        in_specs=(rows, rows, rows, rows, P("dp", None), gain, gain),
        out_specs=(rows, rows, rows, rows, gain, gain),
        check_vma=False,
    )
```
